32 devices in a mesh: section: 2 (over y), ctx: 4 (over z), head: 4 (over x, core).
Axes of the slice: x: 2, y: 2, z: 4, core: 2. Of those that a mesh axis runs over, the one named last changes fastest.
Arguments:
- query: bfloat16 [2, 2048, 8192], P('section', 'ctx', 'head'), may hold values from -30 to 30
- keys: bfloat16 [2, 2048, 1024], P('section', 'ctx', 'head'), may hold values from -6 to 6
- values: bfloat16 [2, 2048, 1024], P('section', 'ctx', 'head'), may hold values from -6 to 6
- attended: bfloat16 [2, 2048, 8192], P('section', 'ctx', 'head'), may hold values from -2 to 2
- output_gradient: bfloat16 [2, 2048, 8192], P('section', 'ctx', 'head'), may hold values from -12 to 12
- segments: int32 [2, 2048], P('section', 'ctx'), may hold values from 0 to 2, as said below
Outputs:
- received_query: float32 [2, 2048, 8192], P('section', 'ctx', 'head')
- received_key: float32 [2, 2048, 1024], P('section', 'ctx', 'head')
- received_value: float32 [2, 2048, 1024], P('section', 'ctx', 'head')
The draws below stay inside these ranges and needn't reach their ends.
Inputs may be any that keep to these rules, and one draw needn't show every extreme that they name: `segments`: document ids never fall with increasing position pos, and every document starts at a position that is a multiple of 64.
All inputs are finite; a program needn't handle non-finite values.
Results may differ from the reference program's by a relative error of at most 0.0057.
Values may be sent and summed in bfloat16 or wider, within the bound.
A program may use at most 128 MiB of HBM per device.

```python
import math
import jax
import jax.numpy as jnp
from jax import lax

HQ = 64
KEY_VALUE_HEADS = 8
HEAD_SIZE = 128
TOK_DEV = 512
QUERY_PER_KV = 8
SEQUENCE_TOKENS = 2048
RELAY_SECTIONS = 2


def joint_rows(key):
    base = jax.random.fold_in(key, 11)
    key_query, random_key_split = jax.random.split(base, 2)
    query_vals = jax.random.truncated_normal(key_query, -6.0, 6.0, (RELAY_SECTIONS, SEQUENCE_TOKENS, HQ * HEAD_SIZE), jnp.float32)
    random_key_values = jax.random.truncated_normal(random_key_split, -6.0, 6.0, (RELAY_SECTIONS, SEQUENCE_TOKENS, KEY_VALUE_HEADS * HEAD_SIZE), jnp.float32)
    return (query_vals, random_key_values)


def draw_query(key, part):
    return joint_rows(key)[0].astype(jnp.bfloat16)


def draw_keys(key, part):
    return joint_rows(key)[1].astype(jnp.bfloat16)


def draw_segments(key, part):
    base = jax.random.fold_in(key, 23)
    key_first, key_last = jax.random.split(base, 2)
    slots = SEQUENCE_TOKENS // 64
    first_cut = 64 * jax.random.randint(key_first, (RELAY_SECTIONS, 1), 1, slots // 4 + 1)
    last_cut = 64 * jax.random.randint(key_last, (RELAY_SECTIONS, 1), slots // 2, 3 * slots // 4 + 1)
    rows = jnp.arange(SEQUENCE_TOKENS, dtype=jnp.int32)
    half = TOK_DEV // 2
    slab = rows // TOK_DEV
    inside = rows % TOK_DEV
    halves = 2 * (SEQUENCE_TOKENS // TOK_DEV)
    where_pos = jnp.where(inside < half, slab * half + inside, (halves - 1 - slab) * half + inside - half)[None, :]
    return ((where_pos >= first_cut).astype(jnp.int32) + (where_pos >= last_cut).astype(jnp.int32)).astype(jnp.int32)


def steps_of(own_key, shape, shards, low, high):
    def one(axis_at, blocks):
        draws = jax.random.uniform(jax.random.fold_in(jax.random.fold_in(own_key, 6), axis_at), (blocks,), jnp.float32, low / len(shards), high / len(shards))
        return jnp.repeat(jnp.exp(draws), shape[axis_at] // blocks).reshape((-1,) + (1,) * (len(shape) - axis_at - 1))

    level = one(*shards[0])
    for cut in shards[1:]:
        level = level * one(*cut)
    return level


def centred(own_key, dims, scale, most, shards=(), kind=jnp.bfloat16):
    result = jax.random.normal(own_key, dims, jnp.float32) * scale
    if len(shards) > 0:
        result = steps_of(own_key, dims, shards, -0.22, 0.18) * result
    return jnp.clip(result, min=-most, max=most).astype(kind)


def setup_inputs(seed: int = 0) -> dict:
    splits = jax.random.split(jax.random.key(seed), 7)
    return {
        "query": draw_query(jax.random.fold_in(splits[6], 71), 0),
        "keys": draw_keys(jax.random.fold_in(splits[6], 71), 0),
        "values": centred(splits[2], (RELAY_SECTIONS, SEQUENCE_TOKENS, KEY_VALUE_HEADS * HEAD_SIZE), 1.0, 6.0, ((0, 2), (1, 4), (2, 4))),
        "attended": centred(splits[3], (RELAY_SECTIONS, SEQUENCE_TOKENS, HQ * HEAD_SIZE), 0.3, 2.0, ((0, 2), (1, 4), (2, 4))),
        "output_gradient": centred(splits[4], (RELAY_SECTIONS, SEQUENCE_TOKENS, HQ * HEAD_SIZE), 2.0, 12.0, ((0, 2), (1, 4), (2, 4))),
        "segments": draw_segments(jax.random.fold_in(splits[6], 71), 0),
    }


def hadamard_table(width):
    indices = jnp.arange(width, dtype=jnp.int32)
    parity = jnp.zeros((width, width), jnp.int32)
    for level in range(width.bit_length() - 1):
        bit_of = jnp.right_shift(indices, level) & 1
        parity = parity + bit_of[:, None] * bit_of[None, :]
    return jnp.where(parity % 2 == 0, 1.0, -1.0).astype(jnp.float32)

def sign_vector(width):
    columns = jnp.arange(width, dtype=jnp.int32)
    return jnp.where((columns * 73 + 41) % 128 < 64, 1.0, -1.0).astype(jnp.float32)

def row_positions():
    rows = jnp.arange(SEQUENCE_TOKENS, dtype=jnp.int32)
    half = TOK_DEV // 2
    slab = rows // TOK_DEV
    inside = rows % TOK_DEV
    halves = 2 * (SEQUENCE_TOKENS // TOK_DEV)
    return jnp.where(inside < half, slab * half + inside, (halves - 1 - slab) * half + inside - half).astype(jnp.int32)

def pack_rows(grads):
    rows, columns = grads.shape
    flipped = (grads.reshape(rows, columns // HEAD_SIZE, HEAD_SIZE) * sign_vector(HEAD_SIZE)).astype(jnp.bfloat16)
    turned = jnp.einsum('rhc,cd->rhd', flipped.astype(jnp.float32), hadamard_table(HEAD_SIZE), precision=lax.Precision.HIGHEST)
    return (turned / math.sqrt(HEAD_SIZE)).reshape(rows, columns).astype(jnp.bfloat16)

def unpack_rows(packed):
    rows, columns = packed.shape
    blocks = packed.astype(jnp.float32).reshape(rows, columns // HEAD_SIZE, HEAD_SIZE)
    turned = jnp.einsum('rhc,cd->rhd', blocks, hadamard_table(HEAD_SIZE), precision=lax.Precision.HIGHEST)
    return (turned / math.sqrt(HEAD_SIZE) * sign_vector(HEAD_SIZE)).reshape(rows, columns)

def section_grads(query, keys, values, attended, output_gradient, segments):
    scale = 1.0 / math.sqrt(HEAD_SIZE)
    query_head_rows = query.astype(jnp.float32).reshape(SEQUENCE_TOKENS, KEY_VALUE_HEADS, QUERY_PER_KV, HEAD_SIZE)
    gradient_heads = output_gradient.astype(jnp.float32).reshape(SEQUENCE_TOKENS, KEY_VALUE_HEADS, QUERY_PER_KV, HEAD_SIZE)
    output_heads = attended.astype(jnp.float32).reshape(SEQUENCE_TOKENS, KEY_VALUE_HEADS, QUERY_PER_KV, HEAD_SIZE)
    key_head_rows = keys.astype(jnp.float32).reshape(SEQUENCE_TOKENS, KEY_VALUE_HEADS, HEAD_SIZE)
    value_head_rows = values.astype(jnp.float32).reshape(SEQUENCE_TOKENS, KEY_VALUE_HEADS, HEAD_SIZE)
    positions = jnp.arange(SEQUENCE_TOKENS, dtype=jnp.int32)
    query_parts, key_section_parts, value_section_parts = ([], [], [])
    for query_group in range(KEY_VALUE_HEADS):
        key_grad = jnp.zeros((SEQUENCE_TOKENS, HEAD_SIZE), jnp.float32)
        value_grad = jnp.zeros((SEQUENCE_TOKENS, HEAD_SIZE), jnp.float32)
        query_rows = []
        for block in range(SEQUENCE_TOKENS // TOK_DEV):
            lower = block * TOK_DEV
            upper = lower + TOK_DEV
            query_block = query_head_rows[lower:upper, query_group]
            grad_block = gradient_heads[lower:upper, query_group]
            out_block = output_heads[lower:upper, query_group]
            keys_group = key_head_rows[:upper, query_group]
            values_group = value_head_rows[:upper, query_group]
            scores = jnp.einsum('qrd,kd->rqk', query_block, keys_group) * scale
            visible = (positions[None, :upper] <= positions[lower:upper, None]) & (segments[None, :upper] == segments[lower:upper, None])
            scores = jnp.where(visible, scores, -1e+30)
            peak = lax.optimization_barrier(jnp.max(scores, axis=-1))
            totals = lax.optimization_barrier(jnp.sum(jnp.where(visible, jnp.exp(scores - peak[..., None]), 0.0), axis=-1))
            lse = peak + jnp.log(totals)
            prob = jnp.exp(scores - lse[..., None])
            prob_low = lax.optimization_barrier(prob.astype(jnp.bfloat16)).astype(jnp.float32)
            dprob = jnp.einsum('qrd,kd->rqk', grad_block, values_group)
            delta = lax.optimization_barrier(jnp.sum(grad_block * out_block, axis=-1)).T
            dscore = prob * (dprob - delta[..., None])
            dscore = lax.optimization_barrier(dscore.astype(jnp.bfloat16)).astype(jnp.float32)
            query_rows.append(jnp.einsum('rqk,kd->qrd', dscore, keys_group) * scale)
            key_grad = key_grad.at[:upper].add(jnp.einsum('rqk,qrd->kd', dscore, query_block) * scale)
            value_grad = value_grad.at[:upper].add(jnp.einsum('rqk,qrd->kd', prob_low, grad_block))
        query_parts.append(jnp.concatenate(query_rows, axis=0))
        key_section_parts.append(key_grad)
        value_section_parts.append(value_grad)
    query_grad = jnp.stack(query_parts, axis=1).reshape(SEQUENCE_TOKENS, HQ * HEAD_SIZE)
    key_gradient_total = jnp.stack(key_section_parts, axis=1).reshape(SEQUENCE_TOKENS, KEY_VALUE_HEADS * HEAD_SIZE)
    value_gradient_total = jnp.stack(value_section_parts, axis=1).reshape(SEQUENCE_TOKENS, KEY_VALUE_HEADS * HEAD_SIZE)
    return (query_grad, key_gradient_total, value_gradient_total)

def reference(query, keys, values, attended, output_gradient, segments):
    where_pos = row_positions()
    order = jnp.zeros((SEQUENCE_TOKENS,), jnp.int32).at[where_pos].set(jnp.arange(SEQUENCE_TOKENS, dtype=jnp.int32))
    packed = []
    for section in range(RELAY_SECTIONS):
        grads = section_grads(query[section][order], keys[section][order], values[section][order], attended[section][order], output_gradient[section][order], segments[section][order])
        packed.append(tuple((pack_rows(item[where_pos]) for item in grads)))
    got_query, got_key, got_value = ([], [], [])
    for section in range(RELAY_SECTIONS):
        source = packed[(section + 1) % RELAY_SECTIONS]
        got_query.append(unpack_rows(source[0]))
        got_key.append(unpack_rows(source[1]))
        got_value.append(unpack_rows(source[2]))
    return (jnp.stack(got_query), jnp.stack(got_key), jnp.stack(got_value))
```

```python
import functools
import math

import jax
import jax.numpy as jnp
import numpy as np
from jax import lax
from jax.experimental import pallas as pl
from jax.experimental.pallas import tpu as pltpu
from jax.sharding import PartitionSpec as P

HEAD = 128
REP = 8
LOG2E = 1.4426950408889634
SCALE = 1.0 / math.sqrt(HEAD)
NEG = -1e30
NT = (((1,), (1,)), ((), ()))
NN = (((1,), (0,)), ((), ()))


def dot(a, b, dims=NN):
    return lax.dot_general(a, b, dims, preferred_element_type=jnp.float32)


def tables():
    idx = np.arange(HEAD)
    parity = np.zeros((HEAD, HEAD), np.int64)
    for level in range(HEAD.bit_length() - 1):
        bit = (idx >> level) & 1
        parity += bit[:, None] * bit[None, :]
    hadamard = np.where(parity % 2 == 0, 1.0, -1.0)
    signs = np.where((idx * 73 + 41) % 128 < 64, 1.0, -1.0)
    return (
        jnp.asarray(hadamard, jnp.bfloat16),
        jnp.asarray(signs[None, :], jnp.float32),
    )


def grads_kernel(
    count, half,
    info, q_ref, g_ref, a_ref, k_ref, v_ref, segq_ref, segk_ref, had_ref, sign_ref,
    out_ref, dkv_ref,
    s_ref, dk_acc, dv_acc, dq_acc, m_ref, l_ref, delta_ref,
):
    slab = 2 * half
    dk_acc[...] = jnp.zeros_like(dk_acc)
    dv_acc[...] = jnp.zeros_like(dv_acc)

    def key_row(j):
        row = jnp.where(j < count, j * slab, (2 * count - 1 - j) * slab + half)
        return pl.multiple_of(row, half)

    def do_half(h, _):
        block = info[h]
        start = info[2 + h]
        rows = pl.ds(pl.multiple_of(h * half, half), half)
        segq = segq_ref[h]
        qpos = block * half + lax.broadcasted_iota(jnp.int32, (1, half), 1)
        m_ref[...] = jnp.full_like(m_ref, NEG)
        l_ref[...] = jnp.zeros_like(l_ref)
        dq_acc[...] = jnp.zeros_like(dq_acc)
        for r in range(REP):
            cols = slice(r * HEAD, (r + 1) * HEAD)
            prod = g_ref[rows, cols].astype(jnp.float32) * a_ref[rows, cols].astype(jnp.float32)
            delta_ref[r] = jnp.sum(prod.T, axis=0, keepdims=True)

        def first(j, _):
            row = pl.ds(key_row(j), half)
            at = pl.ds(pl.multiple_of(j * half, half), half)
            kj = k_ref[row, :]
            kpos = j * half + lax.broadcasted_iota(jnp.int32, (half, 1), 0)
            seen = (kpos <= qpos) & (segk_ref[row, :] == segq)
            bias = jnp.where(seen, 0.0, NEG)
            for r in range(REP):
                qr = q_ref[rows, r * HEAD:(r + 1) * HEAD]
                t = dot(kj, qr, NT) * (SCALE * LOG2E) + bias
                s_ref[r, at, :] = t
                t = t.reshape(half // 8, 8, half)
                m = m_ref[r]
                new = jnp.maximum(m, jnp.max(t, axis=0))
                m_ref[r] = new
                l_ref[r] = l_ref[r] * jnp.exp2(m - new) + jnp.sum(
                    jnp.exp2(t - new[None]), axis=0
                )
            return 0

        lax.fori_loop(start, block + 1, first, 0)
        for r in range(REP):
            m = m_ref[r]
            top = jnp.max(m, axis=0, keepdims=True)
            total = jnp.sum(l_ref[r] * jnp.exp2(m - top), axis=0, keepdims=True)
            m_ref[r, 0:1, :] = top + jnp.log(total) * LOG2E

        def second(j, _):
            row = pl.ds(key_row(j), half)
            at = pl.ds(pl.multiple_of(j * half, half), half)
            kt = k_ref[row, :].astype(jnp.float32).T.astype(jnp.bfloat16)
            vj = v_ref[row, :]
            dk = dk_acc[row, :]
            dv = dv_acc[row, :]
            for r in range(REP):
                cols = slice(r * HEAD, (r + 1) * HEAD)
                qr = q_ref[rows, cols]
                gr = g_ref[rows, cols]
                p = jnp.exp2(s_ref[r, at, :] - m_ref[r, 0:1, :])
                dp = dot(vj, gr, NT)
                ds = (p * (dp - delta_ref[r])).astype(jnp.bfloat16)
                dv = dv + dot(p.astype(jnp.bfloat16), gr)
                dk = dk + dot(ds, qr)
                dq_acc[r] += dot(kt, ds)
            dk_acc[row, :] = dk
            dv_acc[row, :] = dv
            return 0

        lax.fori_loop(start, block + 1, second, 0)
        for r in range(REP):
            dq = dq_acc[r].T * SCALE * sign_ref[...]
            turned = dot(dq.astype(jnp.bfloat16), had_ref[...]) * SCALE
            out_ref[rows, r * HEAD:(r + 1) * HEAD] = turned.astype(jnp.bfloat16)
        return 0

    lax.fori_loop(0, 2, do_half, 0)
    dkv_ref[:, :HEAD] = (dk_acc[...] * SCALE).astype(jnp.bfloat16)
    dkv_ref[:, HEAD:] = dv_acc[...].astype(jnp.bfloat16)


def group_grads(group, count, info, query, grad, att, kv, segq, segk, had, signs):
    tok = query.shape[0]
    half = tok // 2
    total = kv.shape[0]
    wide = REP * HEAD
    whole = lambda i, s: (0, 0)
    mine = lambda i, s: (0, group)
    return pl.pallas_call(
        functools.partial(grads_kernel, count, half),
        out_shape=(
            jax.ShapeDtypeStruct((tok, wide), jnp.bfloat16),
            jax.ShapeDtypeStruct((total, 2 * HEAD), jnp.bfloat16),
        ),
        grid_spec=pltpu.PrefetchScalarGridSpec(
            num_scalar_prefetch=1,
            grid=(1,),
            in_specs=[
                pl.BlockSpec((tok, wide), mine),
                pl.BlockSpec((tok, wide), mine),
                pl.BlockSpec((tok, wide), mine),
                pl.BlockSpec((total, HEAD), lambda i, s: (0, 0)),
                pl.BlockSpec((total, HEAD), lambda i, s: (0, 1)),
                pl.BlockSpec((2, 1, half), lambda i, s: (0, 0, 0)),
                pl.BlockSpec((total, 1), whole),
                pl.BlockSpec((HEAD, HEAD), whole),
                pl.BlockSpec((1, HEAD), whole),
            ],
            out_specs=(
                pl.BlockSpec((tok, wide), whole),
                pl.BlockSpec((total, 2 * HEAD), whole),
            ),
            scratch_shapes=[
                pltpu.VMEM((REP, total, half), jnp.float32),
                pltpu.VMEM((total, HEAD), jnp.float32),
                pltpu.VMEM((total, HEAD), jnp.float32),
                pltpu.VMEM((REP, HEAD, half), jnp.float32),
                pltpu.VMEM((REP, 8, half), jnp.float32),
                pltpu.VMEM((REP, 8, half), jnp.float32),
                pltpu.VMEM((REP, 1, half), jnp.float32),
            ],
        ),
        compiler_params=pltpu.CompilerParams(vmem_limit_bytes=56 * 1024 * 1024),
        cost_estimate=pl.CostEstimate(
            flops=12 * 10**9, bytes_accessed=8 * 10**6, transcendentals=9 * 10**6
        ),
        name="group_grads",
    )(info, query, grad, att, kv, kv, segq, segk, had, signs)


def pack_kernel(parts, *refs):
    had_ref, sign_ref, out_ref = refs[parts:]
    total = refs[0][...].astype(jnp.float32)
    for part in refs[1:parts]:
        total = total + part[...].astype(jnp.float32)
    for c in range(out_ref.shape[1] // HEAD):
        cols = slice(c * HEAD, (c + 1) * HEAD)
        flipped = (total[:, cols] * sign_ref[...]).astype(jnp.bfloat16)
        out_ref[:, cols] = (dot(flipped, had_ref[...]) * SCALE).astype(jnp.bfloat16)


def pack_sum(parts, had, signs):
    return pl.pallas_call(
        functools.partial(pack_kernel, len(parts)),
        out_shape=jax.ShapeDtypeStruct(parts[0].shape, jnp.bfloat16),
        name="pack_sum",
    )(*parts, had, signs)


def unpack_kernel(x_ref, had_ref, sign_ref, *rest):
    out_ref = rest[-1]
    for c in range(out_ref.shape[1] // HEAD):
        cols = slice(c * HEAD, (c + 1) * HEAD)
        out_ref[:, cols] = dot(x_ref[:, cols], had_ref[...]) * SCALE * sign_ref[...]


def unpack_query(packed, group, columns, held, had, signs):
    tok, wide = packed.shape
    part = tok // 2
    specs = [
        pl.BlockSpec((part, wide), lambda i: (i, 0)),
        pl.BlockSpec((HEAD, HEAD), lambda i: (0, 0)),
        pl.BlockSpec((1, HEAD), lambda i: (0, 0)),
    ]
    args = (packed, had, signs)
    alias = {}
    if held is not None:
        specs.append(pl.BlockSpec(memory_space=pl.ANY))
        args = args + (held,)
        alias = {3: 0}
    return pl.pallas_call(
        unpack_kernel,
        out_shape=jax.ShapeDtypeStruct((tok, columns), jnp.float32),
        grid=(2,),
        in_specs=specs,
        out_specs=pl.BlockSpec((part, wide), lambda i: (i, group)),
        input_output_aliases=alias,
        compiler_params=pltpu.CompilerParams(vmem_limit_bytes=32 * 1024 * 1024),
        name="unpack_query",
    )(*args)


def unpack_kv_kernel(groups, *refs):
    had_ref, sign_ref, key_ref, value_ref = refs[groups:]
    for g in range(groups):
        cols = slice(g * HEAD, (g + 1) * HEAD)
        for i, out in enumerate((key_ref, value_ref)):
            part = refs[g][:, i * HEAD:(i + 1) * HEAD]
            out[:, cols] = dot(part, had_ref[...]) * SCALE * sign_ref[...]


def unpack_kv(packed, had, signs):
    tok = packed[0].shape[0]
    shape = jax.ShapeDtypeStruct((tok, len(packed) * HEAD), jnp.float32)
    return pl.pallas_call(
        functools.partial(unpack_kv_kernel, len(packed)),
        out_shape=(shape, shape),
        name="unpack_kv",
    )(*packed, had, signs)


def shift(value, axis, steps):
    count = lax.axis_size(axis)
    pairs = [(source, (source + steps) % count) for source in range(count)]
    return lax.ppermute(value, axis, pairs)


def on_device(query, keys, values, attended, output_gradient, segments):
    query, keys, values = query[0], keys[0], values[0]
    attended, grad, seg = attended[0], output_gradient[0], segments[0]
    tok, columns = query.shape
    half = tok // 2
    groups = keys.shape[1] // HEAD
    count = lax.axis_size("ctx")
    me = lax.axis_index("ctx")
    had, signs = tables()

    seg_all = lax.all_gather(seg, "ctx", axis=0, tiled=True)
    by_half = seg_all.reshape(count, 2, half)
    last = jnp.concatenate([by_half[:, 0, -1], by_half[::-1, 1, -1]])
    starts = [jnp.sum((last < seg[h * half]).astype(jnp.int32)) for h in range(2)]
    info = jnp.stack([me, 2 * count - 1 - me] + starts).astype(jnp.int32)
    segq = seg.reshape(2, 1, half)
    segk = seg_all.reshape(count * tok, 1)

    gathered = []
    for g in range(groups):
        cols = slice(g * HEAD, (g + 1) * HEAD)
        kv = jnp.concatenate([keys[:, cols], values[:, cols]], axis=1)
        if g == 0:
            gathered.append(lax.all_gather(kv, "ctx", axis=0, tiled=True))
        else:
            pieces = [kv] + [shift(kv, "ctx", k) for k in range(1, count)]
            whole = jnp.zeros((count * tok, 2 * HEAD), kv.dtype)
            for k, piece in enumerate(pieces):
                at = (me - k) % count * tok
                whole = lax.dynamic_update_slice(whole, piece, (at, 0))
            gathered.append(whole)

    received, packed_kv = [], []
    for g in range(groups):
        packed, dkv = group_grads(
            g, count, info, query, grad, attended, gathered[g], segq, segk, had, signs
        )
        received.append(shift(packed, "section", -1))
        parts = []
        for k in range(count):
            part = lax.dynamic_slice(dkv, ((me + k) % count * tok, 0), (tok, 2 * HEAD))
            parts.append(part if k == 0 else shift(part, "ctx", k))
        packed_kv.append(shift(pack_sum(parts, had, signs), "section", -1))

    out = None
    for g in range(groups):
        out = unpack_query(received[g], g, columns, out, had, signs)
    out_key, out_value = unpack_kv(packed_kv, had, signs)
    return (out[None], out_key[None], out_value[None])


def solution(mesh):
    spec = P("section", "ctx", "head")
    return jax.shard_map(
        on_device,
        mesh=mesh,
        in_specs=(spec, spec, spec, spec, spec, P("section", "ctx")),
        out_specs=(spec, spec, spec),
        check_vma=False,
    )
```

```python
import functools
import math

import jax
import jax.numpy as jnp
import numpy as np
from jax import lax
from jax.experimental import pallas as pl
from jax.experimental.pallas import tpu as pltpu
from jax.sharding import PartitionSpec as P

HEAD = 128
REP = 8
LOG2E = 1.4426950408889634
SCALE = 1.0 / math.sqrt(HEAD)
NEG = -1e30
NT = (((1,), (1,)), ((), ()))
NN = (((1,), (0,)), ((), ()))


def dot(a, b, dims=NN):
    return lax.dot_general(a, b, dims, preferred_element_type=jnp.float32)


def tables():
    idx = np.arange(HEAD)
    parity = np.zeros((HEAD, HEAD), np.int64)
    for level in range(HEAD.bit_length() - 1):
        bit = (idx >> level) & 1
        parity += bit[:, None] * bit[None, :]
    hadamard = np.where(parity % 2 == 0, 1.0, -1.0)
    signs = np.where((idx * 73 + 41) % 128 < 64, 1.0, -1.0)
    return (
        jnp.asarray(hadamard, jnp.bfloat16),
        jnp.asarray(signs[None, :], jnp.float32),
    )


def mega_kernel(
    count, groups, half, sections,
    q_ref, g_ref, a_ref, k_ref, v_ref, seg_ref, had_ref, sign_ref,
    rq_ref, rkv_ref,
    kv_buf, seg_buf, dkv_out, part, own, q_pack, kv_pack,
    s_ref, dk_acc, dv_acc, dq_acc, m_ref, l_ref, delta_ref,
    kv_send, kv_recv, seg_send, seg_recv, part_send, part_recv,
    q_send, q_recv, back_send, back_recv,
):
    me = lax.axis_index("ctx")
    section = lax.axis_index("section")
    before = lax.rem(section + sections - 1, sections)
    after = lax.rem(section + 1, sections)
    wide = REP * HEAD

    def peer(d):
        return lax.rem(me + d, count)

    def remote(src, dst, send, recv, where):
        return pltpu.make_async_remote_copy(
            src_ref=src, dst_ref=dst, send_sem=send, recv_sem=recv,
            device_id=where, device_id_type=pl.DeviceIdType.MESH,
        )

    def kv_copy(g, h, slab, d, to):
        at = kv_buf.at[g, slab, h]
        return remote(at, at, kv_send.at[g, h, d], kv_recv.at[g, h, slab], {"ctx": to})

    def seg_copy(slab, d, to):
        at = seg_buf.at[slab]
        return remote(at, at, seg_send.at[d], seg_recv.at[slab], {"ctx": to})

    def part_copy(g, h, d, to):
        return remote(
            dkv_out.at[g, to, h], part.at[g, me, h],
            part_send.at[g, h, d], part_recv.at[g, h, me], {"ctx": to},
        )

    def part_arrival(g, h, source):
        at = part.at[g, source, h]
        return remote(at, at, part_send.at[g, h, 0], part_recv.at[g, h, source], {"ctx": source})

    def q_copy(g, h):
        return remote(
            q_pack.at[g, h], rq_ref.at[g, h], q_send.at[g, h], q_recv.at[g, h],
            {"section": before},
        )

    def back_copy(g):
        return remote(
            kv_pack.at[g], rkv_ref.at[g], back_send.at[g], back_recv.at[g],
            {"section": before},
        )

    barrier = pltpu.get_barrier_semaphore()
    for d in range(1, count):
        pl.semaphore_signal(
            barrier, inc=1, device_id={"ctx": peer(d)}, device_id_type=pl.DeviceIdType.MESH
        )
    pl.semaphore_signal(
        barrier, inc=1, device_id={"section": after}, device_id_type=pl.DeviceIdType.MESH
    )
    seg_buf[me] = seg_ref[...]
    for g in range(groups):
        for h in range(2):
            rows = slice(h * half, (h + 1) * half)
            cols = slice(g * HEAD, (g + 1) * HEAD)
            kv_buf[g, me, h, 0] = k_ref[rows, cols]
            kv_buf[g, me, h, 1] = v_ref[rows, cols]
    pl.semaphore_wait(barrier, count)

    for d in range(1, count):
        seg_copy(me, d, peer(d)).start()
    for g in range(groups):
        for d in range(1, count):
            kv_copy(g, 0, me, d, peer(d)).start()
        for d in range(1, count):
            @pl.when(peer(d) < me)
            def _():
                kv_copy(g, 1, me, d, peer(d)).start()

    for d in range(1, count):
        seg_copy(peer(d), d, peer(d)).wait_recv()

    def place(j):
        low = j < count
        return jnp.where(low, j, 2 * count - 1 - j), jnp.where(low, 0, 1)

    def do_group(g):
        base = g * wide
        dk_acc[...] = jnp.zeros_like(dk_acc)
        dv_acc[...] = jnp.zeros_like(dv_acc)

        def do_half(h, _):
            block = jnp.where(h == 0, me, 2 * count - 1 - me)
            rows = pl.ds(pl.multiple_of(h * half, half), half)
            segq = seg_ref[h, 0:1, :]
            qpos = block * half + lax.broadcasted_iota(jnp.int32, (1, half), 1)
            m_ref[...] = jnp.full_like(m_ref, NEG)
            l_ref[...] = jnp.zeros_like(l_ref)
            dq_acc[...] = jnp.zeros_like(dq_acc)
            for r in range(REP):
                cols = slice(base + r * HEAD, base + (r + 1) * HEAD)
                prod = g_ref[rows, cols].astype(jnp.float32) * a_ref[rows, cols].astype(
                    jnp.float32
                )
                delta_ref[r] = jnp.sum(prod.T, axis=0, keepdims=True)

            def first(j, _):
                slab, kh = place(j)
                fresh = jnp.where(h == 0, 0, me + 1)

                @pl.when((j >= fresh) & (j < block))
                def _():
                    kv_copy(g, kh, slab, 0, slab).wait_recv()

                at = pl.ds(pl.multiple_of(j * half, half), half)
                kj = kv_buf[g, slab, kh, 0]
                kpos = j * half + lax.broadcasted_iota(jnp.int32, (half, 1), 0)
                segrow = seg_buf[slab, kh, 0:1, :].astype(jnp.float32)
                segk = jnp.broadcast_to(segrow, (HEAD, half)).T[:, 0:1]
                seen = (kpos <= qpos) & (segk == segq.astype(jnp.float32))
                bias = jnp.where(seen, 0.0, NEG)
                for r in range(REP):
                    qr = q_ref[rows, base + r * HEAD:base + (r + 1) * HEAD]
                    t = dot(kj, qr, NT) * (SCALE * LOG2E) + bias
                    s_ref[r, at, :] = t
                    t = t.reshape(half // 8, 8, half)
                    m = m_ref[r]
                    new = jnp.maximum(m, jnp.max(t, axis=0))
                    m_ref[r] = new
                    l_ref[r] = l_ref[r] * jnp.exp2(m - new) + jnp.sum(
                        jnp.exp2(t - new[None]), axis=0
                    )
                return 0

            lax.fori_loop(0, block + 1, first, 0)
            for r in range(REP):
                m = m_ref[r]
                top = jnp.max(m, axis=0, keepdims=True)
                total = jnp.sum(l_ref[r] * jnp.exp2(m - top), axis=0, keepdims=True)
                m_ref[r, 0:1, :] = top + jnp.log(total) * LOG2E

            def second(j, _):
                slab, kh = place(j)
                at = pl.ds(pl.multiple_of(j * half, half), half)
                kt = kv_buf[g, slab, kh, 0].astype(jnp.float32).T.astype(jnp.bfloat16)
                vj = kv_buf[g, slab, kh, 1]
                dk = dk_acc[slab, kh]
                dv = dv_acc[slab, kh]
                for r in range(REP):
                    cols = slice(base + r * HEAD, base + (r + 1) * HEAD)
                    qr = q_ref[rows, cols]
                    gr = g_ref[rows, cols]
                    p = jnp.exp2(s_ref[r, at, :] - m_ref[r, 0:1, :])
                    dp = dot(vj, gr, NT)
                    ds = (p * (dp - delta_ref[r])).astype(jnp.bfloat16)
                    dv = dv + dot(p.astype(jnp.bfloat16), gr)
                    dk = dk + dot(ds, qr)
                    dq_acc[r] += dot(kt, ds)
                dk_acc[slab, kh] = dk
                dv_acc[slab, kh] = dv
                return 0

            lax.fori_loop(0, block + 1, second, 0)
            for r in range(REP):
                dq = dq_acc[r].T * SCALE * sign_ref[...]
                turned = dot(dq.astype(jnp.bfloat16), had_ref[...]) * SCALE
                q_pack[g, h, :, r * HEAD:(r + 1) * HEAD] = turned.astype(jnp.bfloat16)
            q_copy(g, h).start()
            return 0

        lax.fori_loop(0, 2, do_half, 0)
        for h in range(2):
            own[g, h, 0] = dk_acc[me, h] * SCALE
            own[g, h, 1] = dv_acc[me, h]
            for d in range(1, count):
                to = peer(d)

                def send():
                    dkv_out[g, to, h, 0] = (dk_acc[to, h] * SCALE).astype(jnp.bfloat16)
                    dkv_out[g, to, h, 1] = dv_acc[to, h].astype(jnp.bfloat16)
                    part_copy(g, h, d, to).start()

                if h == 0:
                    send()
                else:
                    pl.when(to > me)(send)

    def finish(g):
        for h in range(2):
            for d in range(1, count):
                source = peer(d)

                def add():
                    part_arrival(g, h, source).wait_recv()
                    own[g, h] += part[g, source, h].astype(jnp.float32)

                if h == 0:
                    add()
                else:
                    pl.when(source < me)(add)
            for i in range(2):
                flipped = (own[g, h, i] * sign_ref[...]).astype(jnp.bfloat16)
                kv_pack[g, h, i] = (dot(flipped, had_ref[...]) * SCALE).astype(jnp.bfloat16)
        back_copy(g).start()

    for g in range(groups):
        do_group(g)
    for g in range(groups):
        finish(g)

    for d in range(1, count):
        seg_copy(me, d, peer(d)).wait_send()
    for g in range(groups):
        for d in range(1, count):
            kv_copy(g, 0, me, d, peer(d)).wait_send()
            part_copy(g, 0, d, peer(d)).wait_send()

            @pl.when(peer(d) < me)
            def _():
                kv_copy(g, 1, me, d, peer(d)).wait_send()

            @pl.when(peer(d) > me)
            def _():
                part_copy(g, 1, d, peer(d)).wait_send()
        for h in range(2):
            q_copy(g, h).wait()
        back_copy(g).wait()


def exchange_grads(count, sections, query, grad, att, keys, values, seg, had, signs):
    tok, columns = query.shape
    half = tok // 2
    groups = keys.shape[1] // HEAD
    wide = REP * HEAD
    vmem = pl.BlockSpec(memory_space=pltpu.VMEM)
    anywhere = pl.BlockSpec(memory_space=pl.ANY)
    low, full = jnp.bfloat16, jnp.float32
    dma = pltpu.SemaphoreType.DMA
    return pl.pallas_call(
        functools.partial(mega_kernel, count, groups, half, sections),
        out_shape=(
            jax.ShapeDtypeStruct((groups, 2, half, wide), low),
            jax.ShapeDtypeStruct((groups, 2, 2, half, HEAD), low),
        ),
        in_specs=[vmem] * 8,
        out_specs=(anywhere, anywhere),
        scratch_shapes=[
            pltpu.VMEM((groups, count, 2, 2, half, HEAD), low),
            pltpu.VMEM((count, 2, 8, half), jnp.int32),
            pltpu.VMEM((groups, count, 2, 2, half, HEAD), low),
            pltpu.VMEM((groups, count, 2, 2, half, HEAD), low),
            pltpu.VMEM((groups, 2, 2, half, HEAD), full),
            pltpu.VMEM((groups, 2, half, wide), low),
            pltpu.VMEM((groups, 2, 2, half, HEAD), low),
            pltpu.VMEM((REP, count * tok, half), full),
            pltpu.VMEM((count, 2, half, HEAD), full),
            pltpu.VMEM((count, 2, half, HEAD), full),
            pltpu.VMEM((REP, HEAD, half), full),
            pltpu.VMEM((REP, 8, half), full),
            pltpu.VMEM((REP, 8, half), full),
            pltpu.VMEM((REP, 1, half), full),
            dma((groups, 2, count)),
            dma((groups, 2, count)),
            dma((count,)),
            dma((count,)),
            dma((groups, 2, count)),
            dma((groups, 2, count)),
            dma((groups, 2)),
            dma((groups, 2)),
            dma((groups,)),
            dma((groups,)),
        ],
        compiler_params=pltpu.CompilerParams(
            vmem_limit_bytes=60 * 1024 * 1024, collective_id=0, has_side_effects=True
        ),
        cost_estimate=pl.CostEstimate(
            flops=24 * 10**9, bytes_accessed=16 * 10**6, transcendentals=18 * 10**6
        ),
        name="exchange_grads",
    )(query, grad, att, keys, values, seg, had, signs)


def unpack_kernel(q_ref, kv_ref, had_ref, sign_ref, out_q, out_k, out_v):
    for c in range(REP):
        cols = slice(c * HEAD, (c + 1) * HEAD)
        out_q[:, cols] = dot(q_ref[0, 0, :, cols], had_ref[...]) * SCALE * sign_ref[...]
    out_k[...] = dot(kv_ref[0, 0, 0], had_ref[...]) * SCALE * sign_ref[...]
    out_v[...] = dot(kv_ref[0, 0, 1], had_ref[...]) * SCALE * sign_ref[...]


def unpack(packed_q, packed_kv, had, signs):
    groups, _, half, wide = packed_q.shape
    shape = lambda width: jax.ShapeDtypeStruct((2 * half, groups * width), jnp.float32)
    block = lambda width: pl.BlockSpec((half, width), lambda g, h: (h, g))
    return pl.pallas_call(
        unpack_kernel,
        out_shape=(shape(wide), shape(HEAD), shape(HEAD)),
        grid=(groups, 2),
        in_specs=[
            pl.BlockSpec((1, 1, half, wide), lambda g, h: (g, h, 0, 0)),
            pl.BlockSpec((1, 1, 2, half, HEAD), lambda g, h: (g, h, 0, 0, 0)),
            pl.BlockSpec((HEAD, HEAD), lambda g, h: (0, 0)),
            pl.BlockSpec((1, HEAD), lambda g, h: (0, 0)),
        ],
        out_specs=(block(wide), block(HEAD), block(HEAD)),
        compiler_params=pltpu.CompilerParams(vmem_limit_bytes=32 * 1024 * 1024),
        name="unpack",
    )(packed_q, packed_kv, had, signs)


def on_device(query, keys, values, attended, output_gradient, segments):
    tok = query.shape[1]
    half = tok // 2
    count = lax.axis_size("ctx")
    sections = lax.axis_size("section")
    had, signs = tables()
    seg = jnp.broadcast_to(segments[0].reshape(2, 1, half), (2, 8, half))
    packed_q, packed_kv = exchange_grads(
        count, sections, query[0], output_gradient[0], attended[0], keys[0], values[0],
        seg, had, signs,
    )
    out_q, out_k, out_v = unpack(packed_q, packed_kv, had, signs)
    return (out_q[None], out_k[None], out_v[None])


def solution(mesh):
    spec = P("section", "ctx", "head")
    return jax.shard_map(
        on_device,
        mesh=mesh,
        in_specs=(spec, spec, spec, spec, spec, P("section", "ctx")),
        out_specs=(spec, spec, spec),
        check_vma=False,
    )
```

```python
import functools
import math

import jax
import jax.numpy as jnp
import numpy as np
from jax import lax
from jax.experimental import pallas as pl
from jax.experimental.pallas import tpu as pltpu
from jax.sharding import PartitionSpec as P

HEAD = 128
REP = 8
LOG2E = 1.4426950408889634
SCALE = 1.0 / math.sqrt(HEAD)
NEG = -1e30
NT = (((1,), (1,)), ((), ()))
NN = (((1,), (0,)), ((), ()))


def dot(a, b, dims=NN):
    return lax.dot_general(a, b, dims, preferred_element_type=jnp.float32)


def tables():
    idx = np.arange(HEAD)
    parity = np.zeros((HEAD, HEAD), np.int64)
    for level in range(HEAD.bit_length() - 1):
        bit = (idx >> level) & 1
        parity += bit[:, None] * bit[None, :]
    hadamard = np.where(parity % 2 == 0, 1.0, -1.0)
    signs = np.where((idx * 73 + 41) % 128 < 64, 1.0, -1.0)
    return (
        jnp.asarray(hadamard, jnp.bfloat16),
        jnp.asarray(signs[None, :], jnp.float32),
    )


def mega_kernel(
    count, groups, half, sections,
    q_hbm, g_hbm, a_hbm, k_ref, v_ref, seg_ref, had_ref, sign_ref,
    rq_ref, rkv_ref,
    q_ref, g_ref, a_ref, kv_buf, seg_buf, dkv_out, part, own, q_pack, kv_pack,
    s_ref, dk_acc, dv_acc, dq_acc, m_ref, l_ref, delta_ref,
    kv_send, kv_recv, seg_send, seg_recv, part_send, part_recv,
    q_send, q_recv, back_send, back_recv, load_sem,
):
    me = lax.axis_index("ctx")
    section = lax.axis_index("section")
    before = lax.rem(section + sections - 1, sections)
    after = lax.rem(section + 1, sections)
    wide = REP * HEAD

    def peer(d):
        return lax.rem(me + d, count)

    def remote(src, dst, send, recv, where):
        return pltpu.make_async_remote_copy(
            src_ref=src, dst_ref=dst, send_sem=send, recv_sem=recv,
            device_id=where, device_id_type=pl.DeviceIdType.MESH,
        )

    def kv_copy(g, h, slab, d, to):
        at = kv_buf.at[g, slab, h]
        return remote(at, at, kv_send.at[g, h, d], kv_recv.at[g, h, slab], {"ctx": to})

    def seg_copy(slab, d, to):
        at = seg_buf.at[slab]
        return remote(at, at, seg_send.at[d], seg_recv.at[slab], {"ctx": to})

    def part_copy(g, h, d, to):
        return remote(
            dkv_out.at[g, to, h], part.at[g, me, h],
            part_send.at[g, h, d], part_recv.at[g, h, me], {"ctx": to},
        )

    def part_arrival(g, h, source):
        at = part.at[g, source, h]
        return remote(at, at, part_send.at[g, h, 0], part_recv.at[g, h, source], {"ctx": source})

    def q_copy(g, h):
        return remote(
            q_pack.at[g, h], rq_ref.at[g, h], q_send.at[g, h], q_recv.at[g, h],
            {"section": before},
        )

    def back_copy(g):
        return remote(
            kv_pack.at[g], rkv_ref.at[g], back_send.at[g], back_recv.at[g],
            {"section": before},
        )

    loads = [
        pltpu.make_async_copy(src, dst, load_sem.at[i])
        for i, (src, dst) in enumerate(((g_hbm, g_ref), (a_hbm, a_ref), (q_hbm, q_ref)))
    ]
    barrier = pltpu.get_barrier_semaphore()
    for d in range(1, count):
        pl.semaphore_signal(
            barrier, inc=1, device_id={"ctx": peer(d)}, device_id_type=pl.DeviceIdType.MESH
        )
    pl.semaphore_signal(
        barrier, inc=1, device_id={"section": after}, device_id_type=pl.DeviceIdType.MESH
    )
    for load in loads:
        load.start()
    for h in range(2):
        seg_buf[me, h] = jnp.broadcast_to(seg_ref[:, h * half:(h + 1) * half], (8, half))
    for g in range(groups):
        for h in range(2):
            rows = slice(h * half, (h + 1) * half)
            cols = slice(g * HEAD, (g + 1) * HEAD)
            kv_buf[g, me, h, 0] = k_ref[rows, cols]
            kv_buf[g, me, h, 1] = v_ref[rows, cols]
    pl.semaphore_wait(barrier, count)

    for d in range(1, count):
        seg_copy(me, d, peer(d)).start()

    def send_keys(g):
        for d in range(1, count):
            kv_copy(g, 0, me, d, peer(d)).start()
        for d in range(1, count):
            @pl.when(peer(d) < me)
            def _():
                kv_copy(g, 1, me, d, peer(d)).start()

    send_keys(0)
    for load in loads:
        load.wait()
    for d in range(1, count):
        seg_copy(peer(d), d, peer(d)).wait_recv()

    def place(j):
        low = j < count
        return jnp.where(low, j, 2 * count - 1 - j), jnp.where(low, 0, 1)

    def finish(g):
        for h in range(2):
            for d in range(1, count):
                source = peer(d)

                def add():
                    part_arrival(g, h, source).wait_recv()
                    own[g, h] += part[g, source, h].astype(jnp.float32)

                if h == 0:
                    add()
                else:
                    pl.when(source < me)(add)
            for i in range(2):
                flipped = (own[g, h, i] * sign_ref[...]).astype(jnp.bfloat16)
                kv_pack[g, h, i] = (dot(flipped, had_ref[...]) * SCALE).astype(jnp.bfloat16)
        back_copy(g).start()

    def do_group(g):
        base = g * wide
        dk_acc[...] = jnp.zeros_like(dk_acc)
        dv_acc[...] = jnp.zeros_like(dv_acc)

        def do_half(h, _):
            block = jnp.where(h == 0, me, 2 * count - 1 - me)
            rows = pl.ds(pl.multiple_of(h * half, half), half)
            segq = seg_buf[me, h, 0:1, :]
            qpos = block * half + lax.broadcasted_iota(jnp.int32, (1, half), 1)
            m_ref[...] = jnp.full_like(m_ref, NEG)
            l_ref[...] = jnp.zeros_like(l_ref)
            dq_acc[...] = jnp.zeros_like(dq_acc)
            for r in range(REP):
                cols = slice(base + r * HEAD, base + (r + 1) * HEAD)
                prod = g_ref[rows, cols].astype(jnp.float32) * a_ref[rows, cols].astype(
                    jnp.float32
                )
                delta_ref[r] = jnp.sum(prod.T, axis=0, keepdims=True)

            def first(j, _):
                slab, kh = place(j)
                fresh = jnp.where(h == 0, 0, me + 1)

                @pl.when((j >= fresh) & (j < block))
                def _():
                    kv_copy(g, kh, slab, 0, slab).wait_recv()

                at = pl.ds(pl.multiple_of(j * half, half), half)
                kj = kv_buf[g, slab, kh, 0]
                kpos = j * half + lax.broadcasted_iota(jnp.int32, (half, 1), 0)
                segrow = seg_buf[slab, kh, 0:1, :].astype(jnp.float32)
                segk = jnp.broadcast_to(segrow, (HEAD, half)).T[:, 0:1]
                seen = (kpos <= qpos) & (segk == segq.astype(jnp.float32))
                bias = jnp.where(seen, 0.0, NEG)
                for r in range(REP):
                    qr = q_ref[rows, base + r * HEAD:base + (r + 1) * HEAD]
                    t = dot(kj, qr, NT) * (SCALE * LOG2E) + bias
                    s_ref[r, at, :] = t
                    t = t.reshape(half // 8, 8, half)
                    m = m_ref[r]
                    new = jnp.maximum(m, jnp.max(t, axis=0))
                    m_ref[r] = new
                    l_ref[r] = l_ref[r] * jnp.exp2(m - new) + jnp.sum(
                        jnp.exp2(t - new[None]), axis=0
                    )
                return 0

            lax.fori_loop(0, block + 1, first, 0)
            if g + 1 < groups:
                pl.when(h == 1)(lambda: send_keys(g + 1))
            for r in range(REP):
                m = m_ref[r]
                top = jnp.max(m, axis=0, keepdims=True)
                total = jnp.sum(l_ref[r] * jnp.exp2(m - top), axis=0, keepdims=True)
                m_ref[r, 0:1, :] = top + jnp.log(total) * LOG2E

            def second(j, _):
                slab, kh = place(j)
                at = pl.ds(pl.multiple_of(j * half, half), half)
                kt = kv_buf[g, slab, kh, 0].astype(jnp.float32).T.astype(jnp.bfloat16)
                vj = kv_buf[g, slab, kh, 1]
                dk = dk_acc[slab, kh]
                dv = dv_acc[slab, kh]
                for r in range(REP):
                    cols = slice(base + r * HEAD, base + (r + 1) * HEAD)
                    qr = q_ref[rows, cols]
                    gr = g_ref[rows, cols]
                    p = jnp.exp2(s_ref[r, at, :] - m_ref[r, 0:1, :])
                    dp = dot(vj, gr, NT)
                    ds = (p * (dp - delta_ref[r])).astype(jnp.bfloat16)
                    dv = dv + dot(p.astype(jnp.bfloat16), gr)
                    dk = dk + dot(ds, qr)
                    dq_acc[r] += dot(kt, ds)
                dk_acc[slab, kh] = dk
                dv_acc[slab, kh] = dv

                @pl.when((h == 1) & (slab != me))
                def _():
                    dkv_out[g, slab, kh, 0] = (dk * SCALE).astype(jnp.bfloat16)
                    dkv_out[g, slab, kh, 1] = dv.astype(jnp.bfloat16)
                    part_copy(g, kh, lax.rem(slab - me + count, count), slab).start()

                return 0

            lax.fori_loop(0, block + 1, second, 0)
            for r in range(REP):
                dq = dq_acc[r].T * SCALE * sign_ref[...]
                turned = dot(dq.astype(jnp.bfloat16), had_ref[...]) * SCALE
                q_pack[g, h, :, r * HEAD:(r + 1) * HEAD] = turned.astype(jnp.bfloat16)
            q_copy(g, h).start()
            if g > 0:
                pl.when(h == 0)(lambda: finish(g - 1))
            return 0

        lax.fori_loop(0, 2, do_half, 0)
        for h in range(2):
            own[g, h, 0] = dk_acc[me, h] * SCALE
            own[g, h, 1] = dv_acc[me, h]

    for g in range(groups):
        do_group(g)
    finish(groups - 1)

    for d in range(1, count):
        seg_copy(me, d, peer(d)).wait_send()
    for g in range(groups):
        for d in range(1, count):
            kv_copy(g, 0, me, d, peer(d)).wait_send()
            part_copy(g, 0, d, peer(d)).wait_send()

            @pl.when(peer(d) < me)
            def _():
                kv_copy(g, 1, me, d, peer(d)).wait_send()

            @pl.when(peer(d) > me)
            def _():
                part_copy(g, 1, d, peer(d)).wait_send()
        for h in range(2):
            q_copy(g, h).wait()
        back_copy(g).wait()


def exchange_grads(count, sections, query, grad, att, keys, values, seg, had, signs):
    tok, columns = query.shape
    half = tok // 2
    groups = keys.shape[1] // HEAD
    wide = REP * HEAD
    vmem = pl.BlockSpec(memory_space=pltpu.VMEM)
    anywhere = pl.BlockSpec(memory_space=pl.ANY)
    low, full = jnp.bfloat16, jnp.float32
    dma = pltpu.SemaphoreType.DMA
    return pl.pallas_call(
        functools.partial(mega_kernel, count, groups, half, sections),
        out_shape=(
            jax.ShapeDtypeStruct((groups, 2, half, wide), low),
            jax.ShapeDtypeStruct((groups, 2, 2, half, HEAD), low),
        ),
        in_specs=[anywhere] * 3 + [vmem] * 5,
        out_specs=(anywhere, anywhere),
        scratch_shapes=[
            pltpu.VMEM((tok, columns), low),
            pltpu.VMEM((tok, columns), low),
            pltpu.VMEM((tok, columns), low),
            pltpu.VMEM((groups, count, 2, 2, half, HEAD), low),
            pltpu.VMEM((count, 2, 8, half), jnp.int32),
            pltpu.VMEM((groups, count, 2, 2, half, HEAD), low),
            pltpu.VMEM((groups, count, 2, 2, half, HEAD), low),
            pltpu.VMEM((groups, 2, 2, half, HEAD), full),
            pltpu.VMEM((groups, 2, half, wide), low),
            pltpu.VMEM((groups, 2, 2, half, HEAD), low),
            pltpu.VMEM((REP, count * tok, half), full),
            pltpu.VMEM((count, 2, half, HEAD), full),
            pltpu.VMEM((count, 2, half, HEAD), full),
            pltpu.VMEM((REP, HEAD, half), full),
            pltpu.VMEM((REP, 8, half), full),
            pltpu.VMEM((REP, 8, half), full),
            pltpu.VMEM((REP, 1, half), full),
            dma((groups, 2, count)),
            dma((groups, 2, count)),
            dma((count,)),
            dma((count,)),
            dma((groups, 2, count)),
            dma((groups, 2, count)),
            dma((groups, 2)),
            dma((groups, 2)),
            dma((groups,)),
            dma((groups,)),
            dma((3,)),
        ],
        compiler_params=pltpu.CompilerParams(
            vmem_limit_bytes=60 * 1024 * 1024, collective_id=0, has_side_effects=True
        ),
        cost_estimate=pl.CostEstimate(
            flops=24 * 10**9, bytes_accessed=16 * 10**6, transcendentals=18 * 10**6
        ),
        name="exchange_grads",
    )(query, grad, att, keys, values, seg, had, signs)


def unpack_kernel(q_ref, kv_ref, had_ref, sign_ref, out_q, out_k, out_v):
    for c in range(REP):
        cols = slice(c * HEAD, (c + 1) * HEAD)
        out_q[:, cols] = dot(q_ref[0, 0, :, cols], had_ref[...]) * SCALE * sign_ref[...]
    out_k[...] = dot(kv_ref[0, 0, 0], had_ref[...]) * SCALE * sign_ref[...]
    out_v[...] = dot(kv_ref[0, 0, 1], had_ref[...]) * SCALE * sign_ref[...]


def unpack(packed_q, packed_kv, had, signs):
    groups, _, half, wide = packed_q.shape
    shape = lambda width: jax.ShapeDtypeStruct((2 * half, groups * width), jnp.float32)
    block = lambda width: pl.BlockSpec((half, width), lambda g, h: (h, g))
    return pl.pallas_call(
        unpack_kernel,
        out_shape=(shape(wide), shape(HEAD), shape(HEAD)),
        grid=(groups, 2),
        in_specs=[
            pl.BlockSpec((1, 1, half, wide), lambda g, h: (g, h, 0, 0)),
            pl.BlockSpec((1, 1, 2, half, HEAD), lambda g, h: (g, h, 0, 0, 0)),
            pl.BlockSpec((HEAD, HEAD), lambda g, h: (0, 0)),
            pl.BlockSpec((1, HEAD), lambda g, h: (0, 0)),
        ],
        out_specs=(block(wide), block(HEAD), block(HEAD)),
        compiler_params=pltpu.CompilerParams(vmem_limit_bytes=60 * 1024 * 1024),
        name="unpack",
    )(packed_q, packed_kv, had, signs)


def on_device(query, keys, values, attended, output_gradient, segments):
    count = lax.axis_size("ctx")
    sections = lax.axis_size("section")
    had, signs = tables()
    packed_q, packed_kv = exchange_grads(
        count, sections, query[0], output_gradient[0], attended[0], keys[0], values[0],
        segments, had, signs,
    )
    out_q, out_k, out_v = unpack(packed_q, packed_kv, had, signs)
    return (out_q[None], out_k[None], out_v[None])


def solution(mesh):
    spec = P("section", "ctx", "head")
    return jax.shard_map(
        on_device,
        mesh=mesh,
        in_specs=(spec, spec, spec, spec, spec, P("section", "ctx")),
        out_specs=(spec, spec, spec),
        check_vma=False,
    )
```

```python
import functools
import math

import jax
import jax.numpy as jnp
import numpy as np
from jax import lax
from jax.experimental import pallas as pl
from jax.experimental.pallas import tpu as pltpu
from jax.sharding import PartitionSpec as P

HEAD = 128
REP = 8
LOG2E = 1.4426950408889634
SCALE = 1.0 / math.sqrt(HEAD)
NEG = -1e30
NT = (((1,), (1,)), ((), ()))
NN = (((1,), (0,)), ((), ()))


def dot(a, b, dims=NN):
    return lax.dot_general(a, b, dims, preferred_element_type=jnp.float32)


def tables():
    idx = np.arange(HEAD)
    parity = np.zeros((HEAD, HEAD), np.int64)
    for level in range(HEAD.bit_length() - 1):
        bit = (idx >> level) & 1
        parity += bit[:, None] * bit[None, :]
    hadamard = np.where(parity % 2 == 0, 1.0, -1.0)
    signs = np.where((idx * 73 + 41) % 128 < 64, 1.0, -1.0)
    return (
        jnp.asarray(hadamard, jnp.bfloat16),
        jnp.asarray(signs[None, :], jnp.float32),
    )


def mega_kernel(
    count, groups, half, sections,
    q_hbm, g_hbm, a_hbm, k_ref, v_ref, seg_ref, had_ref, sign_ref,
    rq_ref, rkv_ref,
    q_ref, g_ref, a_ref, kv_buf, seg_buf, dkv_out, part, own, q_pack, kv_pack,
    s_ref, dk_acc, dv_acc, dq_acc, m_ref, l_ref, delta_ref, top_ref,
    kv_send, kv_recv, seg_send, seg_recv, part_send, part_recv,
    q_send, q_recv, back_send, back_recv, load_sem,
):
    me = lax.axis_index("ctx")
    section = lax.axis_index("section")
    before = lax.rem(section + sections - 1, sections)
    after = lax.rem(section + 1, sections)
    wide = REP * HEAD

    def peer(d):
        return lax.rem(me + d, count)

    def remote(src, dst, send, recv, where):
        return pltpu.make_async_remote_copy(
            src_ref=src, dst_ref=dst, send_sem=send, recv_sem=recv,
            device_id=where, device_id_type=pl.DeviceIdType.MESH,
        )

    def kv_copy(g, h, slab, d, to):
        at = kv_buf.at[g, slab, h]
        return remote(at, at, kv_send.at[g, h, d], kv_recv.at[g, h, slab], {"ctx": to})

    def seg_copy(slab, d, to):
        at = seg_buf.at[slab]
        return remote(at, at, seg_send.at[d], seg_recv.at[slab], {"ctx": to})

    def part_copy(g, h, d, to):
        return remote(
            dkv_out.at[g, to, h], part.at[g, me, h],
            part_send.at[g, h, d], part_recv.at[g, h, me], {"ctx": to},
        )

    def part_arrival(g, h, source):
        at = part.at[g, source, h]
        return remote(at, at, part_send.at[g, h, 0], part_recv.at[g, h, source], {"ctx": source})

    def q_copy(g, h):
        return remote(
            q_pack.at[g, h], rq_ref.at[g, h], q_send.at[g, h], q_recv.at[g, h],
            {"section": before},
        )

    def back_copy(g):
        return remote(
            kv_pack.at[g], rkv_ref.at[g], back_send.at[g], back_recv.at[g],
            {"section": before},
        )

    loads = [
        pltpu.make_async_copy(src, dst, load_sem.at[i])
        for i, (src, dst) in enumerate(((g_hbm, g_ref), (a_hbm, a_ref), (q_hbm, q_ref)))
    ]
    barrier = pltpu.get_barrier_semaphore()
    for d in range(1, count):
        pl.semaphore_signal(
            barrier, inc=1, device_id={"ctx": peer(d)}, device_id_type=pl.DeviceIdType.MESH
        )
    pl.semaphore_signal(
        barrier, inc=1, device_id={"section": after}, device_id_type=pl.DeviceIdType.MESH
    )
    for load in loads:
        load.start()
    for h in range(2):
        seg_buf[me, h] = jnp.broadcast_to(seg_ref[:, h * half:(h + 1) * half], (8, half))
    for g in range(groups):
        for h in range(2):
            rows = slice(h * half, (h + 1) * half)
            cols = slice(g * HEAD, (g + 1) * HEAD)
            kv_buf[g, me, h, 0] = k_ref[rows, cols]
            kv_buf[g, me, h, 1] = v_ref[rows, cols]
    pl.semaphore_wait(barrier, count)

    for d in range(1, count):
        seg_copy(me, d, peer(d)).start()

    def send_keys(g):
        for d in range(1, count):
            kv_copy(g, 0, me, d, peer(d)).start()
        for d in range(1, count):
            @pl.when(peer(d) < me)
            def _():
                kv_copy(g, 1, me, d, peer(d)).start()

    send_keys(0)
    for load in loads:
        load.wait()
    for d in range(1, count):
        seg_copy(peer(d), d, peer(d)).wait_recv()

    def place(j):
        low = j < count
        return jnp.where(low, j, 2 * count - 1 - j), jnp.where(low, 0, 1)

    def finish(g):
        for h in range(2):
            for d in range(1, count):
                source = peer(d)

                def add():
                    part_arrival(g, h, source).wait_recv()
                    own[g, h] += part[g, source, h].astype(jnp.float32)

                if h == 0:
                    add()
                else:
                    pl.when(source < me)(add)
            for i in range(2):
                flipped = (own[g, h, i] * sign_ref[...]).astype(jnp.bfloat16)
                kv_pack[g, h, i] = (dot(flipped, had_ref[...]) * SCALE).astype(jnp.bfloat16)
        back_copy(g).start()

    def do_group(g):
        base = g * wide
        dk_acc[...] = jnp.zeros_like(dk_acc)
        dv_acc[...] = jnp.zeros_like(dv_acc)

        def do_half(h, _):
            block = jnp.where(h == 0, me, 2 * count - 1 - me)
            rows = pl.ds(pl.multiple_of(h * half, half), half)
            segq = seg_buf[me, h, 0:1, :]
            qpos = block * half + lax.broadcasted_iota(jnp.int32, (1, half), 1)
            m_ref[...] = jnp.full_like(m_ref, NEG)
            l_ref[...] = jnp.zeros_like(l_ref)
            dq_acc[...] = jnp.zeros_like(dq_acc)
            for r in range(REP):
                cols = slice(base + r * HEAD, base + (r + 1) * HEAD)
                prod = g_ref[rows, cols].astype(jnp.float32) * a_ref[rows, cols].astype(
                    jnp.float32
                )
                delta_ref[r] = jnp.sum(prod.T, axis=0, keepdims=True)

            def first(i, _):
                j = jnp.where(h == 0, block - i, i)
                slab, kh = place(j)
                fresh = jnp.where(h == 0, 0, me + 1)

                @pl.when((j >= fresh) & (j < block))
                def _():
                    kv_copy(g, kh, slab, 0, slab).wait_recv()

                at = pl.ds(pl.multiple_of(j * half, half), half)
                kj = kv_buf[g, slab, kh, 0]
                kpos = j * half + lax.broadcasted_iota(jnp.int32, (half, 1), 0)
                segrow = seg_buf[slab, kh, 0:1, :].astype(jnp.float32)
                segk = jnp.broadcast_to(segrow, (HEAD, half)).T[:, 0:1]
                seen = (kpos <= qpos) & (segk == segq.astype(jnp.float32))
                bias = jnp.where(seen, 0.0, NEG)
                for r in range(REP):
                    qr = q_ref[rows, base + r * HEAD:base + (r + 1) * HEAD]
                    t = dot(kj, qr, NT) * (SCALE * LOG2E) + bias
                    t = t.reshape(half // 8, 8, half)
                    m = m_ref[r]
                    new = jnp.maximum(m, jnp.max(t, axis=0))
                    m_ref[r] = new
                    top_ref[r, j] = new
                    e = jnp.exp2(t - new[None])
                    s_ref[r, at, :] = e.reshape(half, half)
                    l_ref[r] = l_ref[r] * jnp.exp2(m - new) + jnp.sum(e, axis=0)
                return 0

            lax.fori_loop(0, block + 1, first, 0)
            if g + 1 < groups:
                pl.when(h == 1)(lambda: send_keys(g + 1))
            for r in range(REP):
                m = m_ref[r]
                top = jnp.max(m, axis=0, keepdims=True)
                total = jnp.sum(l_ref[r] * jnp.exp2(m - top), axis=0, keepdims=True)
                m_ref[r, 0:1, :] = top + jnp.log(total) * LOG2E

            def second(j, _):
                slab, kh = place(j)
                at = pl.ds(pl.multiple_of(j * half, half), half)
                kt = kv_buf[g, slab, kh, 0].astype(jnp.float32).T.astype(jnp.bfloat16)
                vj = kv_buf[g, slab, kh, 1]
                dk = dk_acc[slab, kh]
                dv = dv_acc[slab, kh]
                for r in range(REP):
                    cols = slice(base + r * HEAD, base + (r + 1) * HEAD)
                    qr = q_ref[rows, cols]
                    gr = g_ref[rows, cols]
                    f = jnp.exp2(top_ref[r, j] - m_ref[r, 0:1, :])
                    e = s_ref[r, at, :].reshape(half // 8, 8, half)
                    p = (e * f[None]).reshape(half, half)
                    dp = dot(vj, gr, NT)
                    ds = (p * (dp - delta_ref[r])).astype(jnp.bfloat16)
                    dv = dv + dot(p.astype(jnp.bfloat16), gr)
                    dk = dk + dot(ds, qr)
                    dq_acc[r] += dot(kt, ds)
                dk_acc[slab, kh] = dk
                dv_acc[slab, kh] = dv

                @pl.when((h == 1) & (slab != me))
                def _():
                    dkv_out[g, slab, kh, 0] = (dk * SCALE).astype(jnp.bfloat16)
                    dkv_out[g, slab, kh, 1] = dv.astype(jnp.bfloat16)
                    part_copy(g, kh, lax.rem(slab - me + count, count), slab).start()

                return 0

            lax.fori_loop(0, block + 1, second, 0)
            for r in range(REP):
                dq = dq_acc[r].T * SCALE * sign_ref[...]
                turned = dot(dq.astype(jnp.bfloat16), had_ref[...]) * SCALE
                q_pack[g, h, :, r * HEAD:(r + 1) * HEAD] = turned.astype(jnp.bfloat16)
            q_copy(g, h).start()
            if g > 0:
                pl.when(h == 0)(lambda: finish(g - 1))
            return 0

        lax.fori_loop(0, 2, do_half, 0)
        for h in range(2):
            own[g, h, 0] = dk_acc[me, h] * SCALE
            own[g, h, 1] = dv_acc[me, h]

    for g in range(groups):
        do_group(g)
    finish(groups - 1)

    for d in range(1, count):
        seg_copy(me, d, peer(d)).wait_send()
    for g in range(groups):
        for d in range(1, count):
            kv_copy(g, 0, me, d, peer(d)).wait_send()
            part_copy(g, 0, d, peer(d)).wait_send()

            @pl.when(peer(d) < me)
            def _():
                kv_copy(g, 1, me, d, peer(d)).wait_send()

            @pl.when(peer(d) > me)
            def _():
                part_copy(g, 1, d, peer(d)).wait_send()
        for h in range(2):
            q_copy(g, h).wait()
        back_copy(g).wait()


def exchange_grads(count, sections, query, grad, att, keys, values, seg, had, signs):
    tok, columns = query.shape
    half = tok // 2
    groups = keys.shape[1] // HEAD
    wide = REP * HEAD
    vmem = pl.BlockSpec(memory_space=pltpu.VMEM)
    anywhere = pl.BlockSpec(memory_space=pl.ANY)
    low, full = jnp.bfloat16, jnp.float32
    dma = pltpu.SemaphoreType.DMA
    return pl.pallas_call(
        functools.partial(mega_kernel, count, groups, half, sections),
        out_shape=(
            jax.ShapeDtypeStruct((groups, 2, half, wide), low),
            jax.ShapeDtypeStruct((groups, 2, 2, half, HEAD), low),
        ),
        in_specs=[anywhere] * 3 + [vmem] * 5,
        out_specs=(anywhere, anywhere),
        scratch_shapes=[
            pltpu.VMEM((tok, columns), low),
            pltpu.VMEM((tok, columns), low),
            pltpu.VMEM((tok, columns), low),
            pltpu.VMEM((groups, count, 2, 2, half, HEAD), low),
            pltpu.VMEM((count, 2, 8, half), jnp.int32),
            pltpu.VMEM((groups, count, 2, 2, half, HEAD), low),
            pltpu.VMEM((groups, count, 2, 2, half, HEAD), low),
            pltpu.VMEM((groups, 2, 2, half, HEAD), full),
            pltpu.VMEM((groups, 2, half, wide), low),
            pltpu.VMEM((groups, 2, 2, half, HEAD), low),
            pltpu.VMEM((REP, count * tok, half), full),
            pltpu.VMEM((count, 2, half, HEAD), full),
            pltpu.VMEM((count, 2, half, HEAD), full),
            pltpu.VMEM((REP, HEAD, half), full),
            pltpu.VMEM((REP, 8, half), full),
            pltpu.VMEM((REP, 8, half), full),
            pltpu.VMEM((REP, 1, half), full),
            pltpu.VMEM((REP, 2 * count, 8, half), full),
            dma((groups, 2, count)),
            dma((groups, 2, count)),
            dma((count,)),
            dma((count,)),
            dma((groups, 2, count)),
            dma((groups, 2, count)),
            dma((groups, 2)),
            dma((groups, 2)),
            dma((groups,)),
            dma((groups,)),
            dma((3,)),
        ],
        compiler_params=pltpu.CompilerParams(
            vmem_limit_bytes=60 * 1024 * 1024, collective_id=0, has_side_effects=True
        ),
        cost_estimate=pl.CostEstimate(
            flops=24 * 10**9, bytes_accessed=16 * 10**6, transcendentals=18 * 10**6
        ),
        name="exchange_grads",
    )(query, grad, att, keys, values, seg, had, signs)


def unpack_kernel(q_ref, kv_ref, had_ref, sign_ref, out_q, out_k, out_v):
    for c in range(REP):
        cols = slice(c * HEAD, (c + 1) * HEAD)
        out_q[:, cols] = dot(q_ref[0, 0, :, cols], had_ref[...]) * SCALE * sign_ref[...]
    out_k[...] = dot(kv_ref[0, 0, 0], had_ref[...]) * SCALE * sign_ref[...]
    out_v[...] = dot(kv_ref[0, 0, 1], had_ref[...]) * SCALE * sign_ref[...]


def unpack(packed_q, packed_kv, had, signs):
    groups, _, half, wide = packed_q.shape
    shape = lambda width: jax.ShapeDtypeStruct((2 * half, groups * width), jnp.float32)
    block = lambda width: pl.BlockSpec((half, width), lambda g, h: (h, g))
    return pl.pallas_call(
        unpack_kernel,
        out_shape=(shape(wide), shape(HEAD), shape(HEAD)),
        grid=(groups, 2),
        in_specs=[
            pl.BlockSpec((1, 1, half, wide), lambda g, h: (g, h, 0, 0)),
            pl.BlockSpec((1, 1, 2, half, HEAD), lambda g, h: (g, h, 0, 0, 0)),
            pl.BlockSpec((HEAD, HEAD), lambda g, h: (0, 0)),
            pl.BlockSpec((1, HEAD), lambda g, h: (0, 0)),
        ],
        out_specs=(block(wide), block(HEAD), block(HEAD)),
        compiler_params=pltpu.CompilerParams(vmem_limit_bytes=60 * 1024 * 1024),
        name="unpack",
    )(packed_q, packed_kv, had, signs)


def on_device(query, keys, values, attended, output_gradient, segments):
    count = lax.axis_size("ctx")
    sections = lax.axis_size("section")
    had, signs = tables()
    packed_q, packed_kv = exchange_grads(
        count, sections, query[0], output_gradient[0], attended[0], keys[0], values[0],
        segments, had, signs,
    )
    out_q, out_k, out_v = unpack(packed_q, packed_kv, had, signs)
    return (out_q[None], out_k[None], out_v[None])


def solution(mesh):
    spec = P("section", "ctx", "head")
    return jax.shard_map(
        on_device,
        mesh=mesh,
        in_specs=(spec, spec, spec, spec, spec, P("section", "ctx")),
        out_specs=(spec, spec, spec),
        check_vma=False,
    )
```
